32 devices in a mesh: sim: 16 (over z, y, x), lens: 2 (over core).
Axes of the slice: x: 2, y: 2, z: 4, core: 2. Of those that a mesh axis runs over, the one named last changes fastest.
Arguments:
- patches: bfloat16 [4096, 2, 2048], P(('sim', 'lens')), may hold values from -6 to 6
- patch_cycle: int32 [4096, 1], P(('sim', 'lens')), may hold values from 0 to 15; in each aligned block of 128 rows (0 to 127, 128 to 255, ...) at most 16 rows name the same one
- patch_block: int32 [4096], P(('sim', 'lens')), may hold values from 0 to 7
- m_values: int32 [32], replicated, may hold values from 0 to 8191, as said below
- shell_weight: float32 [2], replicated, may hold values from 0.5 to 2
- legendre_panel: bfloat16 [32, 32, 8192], P('sim', 'lens'), as said below
- spin2_panel: bfloat16 [32, 32, 8192], P('sim', 'lens'), as said below
Outputs:
- kappa_modes: float32 [32, 2, 32], P('sim', None, 'lens')
- shear_modes: float32 [32, 2, 32], P('sim', None, 'lens')
The draws below stay inside these ranges and needn't reach their ends.
Inputs may be any that keep to these rules, and one draw needn't show every extreme that they name: `patch_cycle`: among the 128 patches of one device, at most 16 lie on one cycle; some device reaches 16. `m_values`: the 32 orders are distinct; slots 2 d and 2 d + 1 hold m and 8191 - m with m below 4096, and some sim index holds 0 and 8191. legendre_panel[j, g, l] is 0 for l < 128 * (m_values[j] // 128). spin2_panel[j, g, l] is 0 for l < 128 * (m_values[j] // 128).
All inputs are finite; a program needn't handle non-finite values.
Results may differ from the reference program's by a relative error of at most 0.014.
Values may be sent and summed in bfloat16 or wider, within the bound.
No kernel may reach another device: no remote copies, remote signals or barrier semaphores. Data moves between devices by JAX's collectives and lax.ppermute only.
A program may use at most 64 MiB of HBM per device.

```python
import math
import jax
import jax.numpy as jnp
import numpy as np
from jax import lax

NPIX = 16384
BPX = 2048
LMAX = 8192
LB = 128
SHELLS = 2
K_DEV = 128
NBLK = 8
CAP = 16
MW = 32
CYCLES = 32
PATCHES = 4096
N_SIM = 16
N_LENS = 2


def order_table(key):
    half = LMAX // 2
    others = jax.random.permutation(jax.random.fold_in(key, 7), half - 1)[:N_SIM - 1] + 1
    small = jnp.concatenate([jnp.array([0], jnp.int32), others.astype(jnp.int32)])
    small = jax.random.permutation(jax.random.fold_in(key, 8), small)
    pairs = jnp.stack([small, LMAX - 1 - small], axis=1)
    return pairs.reshape(-1).astype(jnp.int32)


def panel_values(key, salt):
    orders = order_table(key)
    ell = jnp.arange(LMAX, dtype=jnp.int32)
    keep = (ell[None, :] >= LB * (orders // LB)[:, None]).astype(jnp.float32)
    inner_key = jax.random.fold_in(key, salt)
    values = jax.random.normal(inner_key, (MW, CYCLES, LMAX), jnp.float32)
    return (values * keep[:, None, :]).astype(jnp.bfloat16)


def draw_m_values(key, part):
    return order_table(key)


def draw_legendre_panel(key, part):
    return panel_values(key, 21)


def draw_spin2_panel(key, part):
    return panel_values(key, 22)


def touch_ends(result, rng, low, high):
    longest = result.shape.index(max(result.shape))
    spots = []
    for shift in (0, 1):
        where = [jax.random.randint(jax.random.fold_in(rng, axis), (), 0, length) for axis, length in enumerate(result.shape)]
        where[longest] = (where[longest] + shift) % result.shape[longest]
        spots.append(tuple(where))
    return result.at[spots[0]].set(low).at[spots[1]].set(high)


def block_scale(stream_key, dims, pieces, least, top_value):
    def one(position, blocks):
        draws = jax.random.uniform(jax.random.fold_in(jax.random.fold_in(stream_key, 6), position), (blocks,), jnp.float32, least / len(pieces), top_value / len(pieces))
        return jnp.repeat(jnp.exp(draws), dims[position] // blocks).reshape((-1,) + (1,) * (len(dims) - position - 1))

    factor_of = one(*pieces[0])
    for cut in pieces[1:]:
        factor_of = factor_of * one(*cut)
    return factor_of


def shared_out(own_key, own, number, rows, count, top, most, slope):
    sequence = jax.random.permutation(own_key, count)
    crowded, usual = portions_of(count, rows * top, most, slope, True), portions_of(count, rows * top, most, slope, False)
    places = jnp.arange(count)

    def named(sizes, offset_by):
        used = int((sizes > 0).sum())
        fixed = max(1, used // 4)
        moved = fixed + (places - fixed + offset_by * (used - fixed)) % max(1, count - fixed)
        return jnp.zeros((count,), jnp.int32).at[sequence[jnp.where(places < fixed, places, moved)]].set(jnp.asarray(sizes, jnp.int32))

    sizes = jnp.where(number % 4 == 0, named(crowded, number // 4), named(usual, number - number // 4 - 1))
    mixed = jax.random.permutation(jax.random.fold_in(own, 3), count)
    donor, sink = mixed[0:count // 2 * 2:2], mixed[1:count // 2 * 2:2]
    room = jnp.minimum(sizes[donor] - 1, most - sizes[sink]) // 2
    room = jnp.where((donor == sequence[0]) | (sink == sequence[0]) | (sizes[sink] == 0), 0, jnp.maximum(room, 0))
    moved = jax.random.randint(jax.random.fold_in(own, 4), (count // 2,), 0, 1 << 20) % (room + 1)
    sizes = sizes.at[donor].add(-moved).at[sink].add(moved)
    labels = jnp.searchsorted(jnp.cumsum(sizes), jnp.arange(rows * top), side="right").astype(jnp.int32)
    listing = labels.reshape(top, rows).T
    listing = listing[jax.random.permutation(jax.random.fold_in(own, 1), rows)]
    offset_by = jax.random.randint(jax.random.fold_in(own, 2), (rows, 1), 0, top)
    return jnp.take_along_axis(listing, (jnp.arange(top)[None, :] + offset_by) % top, axis=1)


def portions_of(number_of, total, limit, slope, full):
    loads = [(1 << 20) // math.isqrt(grade ** slope) + 1 for grade in range(1, number_of + 1)]
    largest = limit if full else min(limit, max(-(-total // number_of), total * loads[0] // sum(loads)))
    least = 1 if total - largest >= number_of - 1 else 0
    holding, rest = [largest] + [least] * (number_of - 1), total - largest - least * (number_of - 1)
    while rest > 0:
        free = [i for i in range(1, number_of) if holding[i] < largest] or [i for i in range(1, number_of) if holding[i] < limit]
        pool, remaining = sum([loads[i] for i in free]), rest
        for i in free:
            more = min(limit - holding[i], max(1, remaining * loads[i] // pool), rest)
            holding[i] = holding[i] + more
            rest = rest - more
    return np.array(holding)


def centred(key, dims, spread, limit, cuts=(), held_as=jnp.bfloat16):
    values = spread * jax.random.normal(key, dims, jnp.float32)
    if cuts:
        values = values * block_scale(key, dims, cuts, -0.22, 0.18)
    return jnp.clip(values, -limit, limit).astype(held_as)


def setup_inputs(seed: int = 0) -> dict:
    key_list = jax.random.split(jax.random.key(seed), 8)
    patches = centred(key_list[0], (PATCHES, SHELLS, BPX), 1.0, 6.0, ((0, 32),))
    patch_cycle_keys = jax.random.split(jax.random.fold_in(key_list[1], 1), PATCHES // K_DEV)
    patch_cycle_turns = jax.random.permutation(jax.random.fold_in(key_list[1], 3), PATCHES // K_DEV)
    patch_cycle = jax.vmap(lambda own, number: shared_out(jax.random.fold_in(key_list[1], 2), own, number, K_DEV, N_SIM, 1, CAP, 2))(patch_cycle_keys, patch_cycle_turns).reshape((PATCHES, 1))
    patch_block = touch_ends(jax.random.randint(key_list[2], (PATCHES,), 0, NBLK), jax.random.fold_in(key_list[2], 1), 0, NBLK - 1).astype(jnp.int32)
    m_values = draw_m_values(jax.random.fold_in(key_list[7], 71), 0)
    shell_weight = jnp.clip(jnp.exp(jax.random.uniform(key_list[4], (SHELLS,), jnp.float32, math.log(0.5), math.log(2.0))), 0.5, 2.0)
    legendre_panel = draw_legendre_panel(jax.random.fold_in(key_list[7], 71), 0)
    spin2_panel = draw_spin2_panel(jax.random.fold_in(key_list[7], 71), 0)
    return {"patches": patches, "patch_cycle": patch_cycle, "patch_block": patch_block, "m_values": m_values, "shell_weight": shell_weight, "legendre_panel": legendre_panel, "spin2_panel": spin2_panel}


def cycle_table(m_values, parity):
    pixel = jnp.arange(NPIX, dtype=jnp.int32)
    angle_index = (2 * pixel[:, None] * m_values[None, :] + parity * m_values[None, :]) % (2 * NPIX)
    angle = angle_index.astype(jnp.float32) * (math.pi / NPIX)
    return jnp.concatenate([jnp.cos(angle), jnp.sin(angle)], axis=1)

def reference(patches, patch_cycle, patch_block, m_values, shell_weight, legendre_panel, spin2_panel):
    cycles = N_SIM * N_LENS
    device = jnp.arange(K_DEV * N_SIM * N_LENS, dtype=jnp.int32) // K_DEV
    column = device % N_LENS
    cycle_global = column * N_SIM + patch_cycle[:, 0]
    segment = cycle_global * NBLK + patch_block
    density = jax.ops.segment_sum(patches.astype(jnp.float32), segment, num_segments=cycles * NBLK)
    density = density.reshape(cycles, NBLK, SHELLS, BPX).transpose(0, 2, 1, 3).reshape(cycles, SHELLS, NPIX)
    halves = []
    for parity in range(2):
        rows = density[parity::2].reshape(-1, NPIX)
        sums = jnp.dot(rows, cycle_table(m_values, parity), precision=lax.Precision.HIGHEST)
        halves.append(sums.reshape(cycles // 2, SHELLS, 2, MW))
    sums = jnp.stack(halves, axis=1).reshape(cycles, SHELLS, 2, MW)
    modes = jnp.stack([sums[:, :, 0], -sums[:, :, 1]], axis=2) / math.sqrt(NPIX)
    modes_rounded = modes.astype(jnp.bfloat16).reshape(cycles, SHELLS * 2, MW).transpose(2, 0, 1)

    def analyse(items):
        panel, coeffs = items
        return jnp.dot(coeffs.T, panel, preferred_element_type=jnp.float32)
    delta = lax.map(analyse, (legendre_panel, modes_rounded)).reshape(MW, SHELLS, 2, LMAX)
    kappa = jnp.zeros((MW, 2, LMAX), jnp.float32)
    for shell in range(SHELLS):
        kappa = kappa + shell_weight[shell] * delta[:, shell]
    kappa = kappa / math.sqrt(cycles)
    ell = jnp.arange(LMAX, dtype=jnp.int32).astype(jnp.float32)
    factor = jnp.where(ell >= 2.0, jnp.sqrt((ell + 2.0) * (ell - 1.0) / jnp.maximum(ell * (ell + 1.0), 1.0)), 0.0)
    shear = kappa * factor
    kappa_rounded = kappa.astype(jnp.bfloat16)
    shear_rounded = shear.astype(jnp.bfloat16)

    def synthesise(items):
        spin_zero, spin_two, kappa_row, shear_row = items
        return (jnp.dot(kappa_row, spin_zero.T, preferred_element_type=jnp.float32), jnp.dot(shear_row, spin_two.T, preferred_element_type=jnp.float32))
    kappa_modes, shear_modes = lax.map(synthesise, (legendre_panel, spin2_panel, kappa_rounded, shear_rounded))
    scale = 1.0 / math.sqrt(LMAX)
    return (kappa_modes * scale, shear_modes * scale)
```

```python
import math

import jax
import jax.numpy as jnp
from jax import lax
from jax.experimental import pallas as pl
from jax.experimental.pallas import tpu as pltpu
from jax.sharding import PartitionSpec as P

NPIX = 16384
NT = (((1,), (1,)), ((), ()))


def cos_sin(index, turn):
    quarter = turn // 4
    quadrant = (index + quarter // 2) // quarter
    r = (index - quadrant * quarter).astype(jnp.float32) * (2.0 * math.pi / turn)
    q = r * r
    sine = r + r * q * (-1.0 / 6 + q * (1.0 / 120 + q * (-1.0 / 5040 + q * (1.0 / 362880))))
    cosine = 1.0 + q * (-0.5 + q * (1.0 / 24 + q * (-1.0 / 720 + q * (1.0 / 40320))))
    odd = (quadrant & 1) == 1
    c = jnp.where(odd, sine, cosine)
    s = jnp.where(odd, cosine, sine)
    c = jnp.where(((quadrant + 1) & 2) == 2, -c, c)
    s = jnp.where((quadrant & 2) == 2, -s, s)
    return c, s


def split(x):
    high = x.astype(jnp.bfloat16)
    return high, (x - high.astype(jnp.float32)).astype(jnp.bfloat16)


def iota(shape, dim):
    return lax.broadcasted_iota(jnp.int32, shape, dim)


def terms_kernel(m_ref, cycle_ref, block_ref, patch_ref, out_ref):
    number, shells, bpx = patch_ref.shape
    orders = m_ref.shape[1]
    n_sim = lax.axis_size("sim")
    m_dev = orders // n_sim
    cycles = n_sim * lax.axis_size("lens")
    rank = lax.axis_index("sim")
    square = (orders, orders)
    row = iota(square, 0)
    slot = ((row // m_dev) ^ rank) * m_dev + row % m_dev
    m_row = m_ref[...].astype(jnp.float32)
    m_col = jnp.sum(jnp.where(slot == iota(square, 1), m_row, 0.0), axis=1, keepdims=True)
    m_col = m_col.astype(jnp.int32)
    low_c, low_s = cos_sin((m_col * iota((orders, 128), 1)) & (NPIX - 1), NPIX)
    parts = bpx // 128
    high_c, high_s = cos_sin((m_col * (128 * iota((orders, 128), 1))) & (NPIX - 1), NPIX)
    rows = number * shells
    total = jnp.zeros((4 * orders, rows), jnp.float32)
    for part in range(parts):
        hc = high_c[:, part : part + 1]
        hs = high_s[:, part : part + 1]
        c_high, c_low = split(low_c * hc - low_s * hs)
        s_high, s_low = split(low_s * hc + low_c * hs)
        table = jnp.concatenate([c_high, s_high, c_low, s_low], axis=0)
        chunk = patch_ref[:, :, part * 128 : (part + 1) * 128].reshape(rows, 128)
        total += lax.dot_general(table, chunk, NT, preferred_element_type=jnp.float32)
    total = total[: 2 * orders] + total[2 * orders :]
    cosine, sine = total[:orders], total[orders:]
    where = jnp.where(iota((8, number), 0) == 0, block_ref[...], cycle_ref[...])
    spread = (iota((number, rows), 1) // shells == iota((number, rows), 0)).astype(jnp.bfloat16)
    where = jnp.dot(
        where.astype(jnp.float32).astype(jnp.bfloat16), spread, preferred_element_type=jnp.float32
    ).astype(jnp.int32)
    block = where[0:1]
    cycle = where[1:2] + lax.axis_index("lens") * n_sim
    phase = 2 * bpx * block + (cycle & 1)
    turn_c, turn_s = cos_sin((m_col * phase) & (2 * NPIX - 1), 2 * NPIX)
    real, imag = turn_c * cosine - turn_s * sine, -(turn_s * cosine + turn_c * sine)
    pick = shells * cycles
    line, lane = iota((pick, rows), 0), iota((pick, rows), 1)
    chosen = (line == (lane % shells) * cycles + cycle).astype(jnp.bfloat16)
    r_high, r_low = split(real)
    i_high, i_low = split(imag)
    stacked = jnp.concatenate([r_high, i_high, r_low, i_low], axis=0)
    summed = lax.dot_general(stacked, chosen, NT, preferred_element_type=jnp.float32)
    summed = summed[: 2 * orders] + summed[2 * orders :]
    out_ref[...] = jnp.concatenate([summed[:orders], summed[orders:]], axis=1)


def fourier_terms(patches, patch_cycle, patch_block, m_values):
    number, shells, bpx = patches.shape
    orders = m_values.shape[0]
    cycles = lax.axis_size("sim") * lax.axis_size("lens")
    return pl.pallas_call(
        terms_kernel,
        out_shape=jax.ShapeDtypeStruct((orders, 2 * shells * cycles), jnp.float32),
        compiler_params=pltpu.CompilerParams(vmem_limit_bytes=48 << 20),
        name="fourier_terms",
    )(m_values.reshape(1, -1), patch_cycle.reshape(1, -1), patch_block.reshape(1, -1), patches)


def gram_kernel(own_ref, spin_ref, *refs):
    other_refs, out_ref = refs[:-1], refs[-1]
    m_dev, rows, lmax = own_ref.shape
    n_lens = lax.axis_size("lens")
    rank = lax.axis_index("lens")
    ell = iota((8, lmax), 1).astype(jnp.float32)
    factor = jnp.where(
        ell >= 2.0, jnp.sqrt((ell + 2.0) * (ell - 1.0) / jnp.maximum(ell * (ell + 1.0), 1.0)), 0.0
    )[0:1]
    for slot in range(m_dev):
        shear = (spin_ref[slot].astype(jnp.float32) * factor).astype(jnp.bfloat16)
        left = jnp.concatenate([own_ref[slot], shear], axis=0)
        right = jnp.concatenate([own_ref[slot]] + [r[slot] for r in other_refs], axis=0)
        gram = lax.dot_general(left, right, NT, preferred_element_type=jnp.float32)
        columns = []
        for column in range(n_lens):
            value = gram[:, :rows]
            for step in range(1, n_lens):
                value = jnp.where(
                    rank ^ step == column, gram[:, step * rows : (step + 1) * rows], value
                )
            columns.append(value)
        out_ref[slot] = jnp.concatenate(columns, axis=1)


def gram_matrices(own, spin, others):
    m_dev, rows, lmax = own.shape
    cycles = rows * lax.axis_size("lens")
    read = 2 * own.size * (2 + len(others))
    return pl.pallas_call(
        gram_kernel,
        out_shape=jax.ShapeDtypeStruct((m_dev, 2 * rows, cycles), jnp.float32),
        compiler_params=pltpu.CompilerParams(vmem_limit_bytes=48 << 20),
        cost_estimate=pl.CostEstimate(
            flops=4 * m_dev * rows * cycles * lmax, bytes_accessed=read, transcendentals=0
        ),
        name="gram_matrices",
    )(own, spin, *others)


def output_kernel(scale, weight_ref, modes_ref, gram_ref, kappa_ref, shear_ref):
    m_dev, _, cycles = gram_ref.shape
    rows = kappa_ref.shape[2]
    shells = weight_ref.shape[0]
    for slot in range(m_dev):
        modes = modes_ref[slot : slot + 1]
        parts = []
        for part in range(2):
            value = jnp.zeros((1, cycles), jnp.float32)
            for shell in range(shells):
                at = (part * shells + shell) * cycles
                value += modes[:, at : at + cycles] * (weight_ref[shell] * scale)
            parts.append(value)
        both = lax.dot_general(
            jnp.concatenate(parts, axis=0),
            gram_ref[slot],
            NT,
            precision=lax.Precision.HIGHEST,
            preferred_element_type=jnp.float32,
        )
        kappa_ref[slot] = both[:, :rows]
        shear_ref[slot] = both[:, rows:]


def outputs(weight, modes, gram, rows, scale):
    m_dev = gram.shape[0]
    shape = jax.ShapeDtypeStruct((m_dev, 2, rows), jnp.float32)
    vmem = pl.BlockSpec(memory_space=pltpu.VMEM)
    return pl.pallas_call(
        lambda *refs: output_kernel(scale, *refs),
        out_shape=(shape, shape),
        in_specs=[pl.BlockSpec(memory_space=pltpu.SMEM), vmem, vmem],
        out_specs=(vmem, vmem),
        compiler_params=pltpu.CompilerParams(vmem_limit_bytes=48 << 20),
        name="outputs",
    )(weight, modes, gram)


def on_device(
    patches, patch_cycle, patch_block, m_values, shell_weight, legendre_panel, spin2_panel
):
    n_sim = lax.axis_size("sim")
    n_lens = lax.axis_size("lens")
    m_dev, rows, lmax = legendre_panel.shape

    def swap(x, mask):
        pairs = [(i, i ^ mask) for i in range(n_sim * n_lens)]
        return lax.ppermute(x, ("sim", "lens"), pairs)

    others = [swap(legendre_panel, step) for step in range(1, n_lens)]
    terms = fourier_terms(patches, patch_cycle, patch_block, m_values)
    step = 1
    while step < n_lens:
        terms = terms + swap(terms, step)
        step *= 2
    gram = gram_matrices(legendre_panel, spin2_panel, others)
    half = n_sim // 2
    while half >= 1:
        kept = half * m_dev
        terms = terms[:kept] + swap(terms[kept:], half * n_lens + (1 if n_lens > 1 else 0))
        half //= 2
    scale = 1.0 / math.sqrt(NPIX * n_sim * n_lens * lmax)
    return outputs(shell_weight, terms, gram, rows, scale)


def solution(mesh):
    placed = (
        P(("sim", "lens"), None, None),
        P(("sim", "lens"), None),
        P(("sim", "lens")),
        P(),
        P(),
        P("sim", "lens", None),
        P("sim", "lens", None),
    )
    return jax.shard_map(
        on_device,
        mesh=mesh,
        in_specs=placed,
        out_specs=(P("sim", None, "lens"), P("sim", None, "lens")),
        check_vma=False,
    )
```

```python
import math

import jax
import jax.numpy as jnp
from jax import lax
from jax.experimental import pallas as pl
from jax.experimental.pallas import tpu as pltpu
from jax.sharding import PartitionSpec as P

NPIX = 16384
NT = (((1,), (1,)), ((), ()))
PIECES = 1


def cos_sin(index, turn):
    quarter = turn // 4
    quadrant = (index + quarter // 2) // quarter
    r = (index - quadrant * quarter).astype(jnp.float32) * (2.0 * math.pi / turn)
    q = r * r
    sine = r + r * q * (-1.0 / 6 + q * (1.0 / 120 + q * (-1.0 / 5040 + q * (1.0 / 362880))))
    cosine = 1.0 + q * (-0.5 + q * (1.0 / 24 + q * (-1.0 / 720 + q * (1.0 / 40320))))
    odd = (quadrant & 1) == 1
    c = jnp.where(odd, sine, cosine)
    s = jnp.where(odd, cosine, sine)
    c = jnp.where(((quadrant + 1) & 2) == 2, -c, c)
    s = jnp.where((quadrant & 2) == 2, -s, s)
    return c, s


def split(x):
    high = x.astype(jnp.bfloat16)
    return high, (x - high.astype(jnp.float32)).astype(jnp.bfloat16)


def iota(shape, dim):
    return lax.broadcasted_iota(jnp.int32, shape, dim)


def terms_kernel(
    scale, m_hbm, cycle_hbm, block_hbm, weight_hbm, patch_hbm, out_ref,
    m_ref, cycle_ref, block_ref, weight_ref, patch_ref, table_ref, small_sem, patch_sem
):
    number, shells, bpx = patch_ref.shape
    orders = m_ref.shape[1]
    n_sim = lax.axis_size("sim")
    m_dev = orders // n_sim
    small = [
        pltpu.make_async_copy(source, target, small_sem.at[i])
        for i, (source, target) in enumerate(
            ((m_hbm, m_ref), (cycle_hbm, cycle_ref), (block_hbm, block_ref), (weight_hbm, weight_ref))
        )
    ]
    width = bpx // PIECES
    large = [
        pltpu.make_async_copy(
            patch_hbm.at[:, :, pl.ds(i * width, width)],
            patch_ref.at[:, :, pl.ds(i * width, width)],
            patch_sem.at[i],
        )
        for i in range(PIECES)
    ]
    for copy in small + large:
        copy.start()
    square = (orders, orders)
    row = iota(square, 0)
    slot = (row % n_sim) * m_dev + row // n_sim
    for copy in small:
        copy.wait()
    m_row = m_ref[...].astype(jnp.float32)
    m_col = jnp.sum(jnp.where(slot == iota(square, 1), m_row, 0.0), axis=1, keepdims=True)
    m_col = m_col.astype(jnp.int32)
    low_c, low_s = cos_sin((m_col * iota((orders, 128), 1)) & (NPIX - 1), NPIX)
    parts = bpx // 128
    high_c, high_s = cos_sin((m_col * (128 * iota((orders, 128), 1))) & (NPIX - 1), NPIX)
    rows = number * shells
    where = jnp.where(iota((8, number), 0) == 0, block_ref[...], cycle_ref[...])
    spread = (iota((number, rows), 1) // shells == iota((number, rows), 0)).astype(jnp.bfloat16)
    where = jnp.dot(
        where.astype(jnp.float32).astype(jnp.bfloat16), spread, preferred_element_type=jnp.float32
    ).astype(jnp.int32)
    block, cycle = where[0:1], where[1:2]
    parity = (cycle + lax.axis_index("lens") * n_sim) & 1
    phase = 2 * bpx * block + parity
    turn_c, turn_s = cos_sin((m_col * phase) & (2 * NPIX - 1), 2 * NPIX)
    lane = iota((1, rows), 1) % shells
    weight = jnp.zeros((1, rows), jnp.float32)
    for shell in range(shells):
        weight = jnp.where(lane == shell, weight_ref[0:1, shell : shell + 1] * scale, weight)
    turn_c, turn_s = turn_c * weight, turn_s * weight
    chosen = (iota((n_sim, rows), 0) == cycle).astype(jnp.bfloat16)
    for part in range(parts):
        hc = high_c[:, part : part + 1]
        hs = high_s[:, part : part + 1]
        c_high, c_low = split(low_c * hc - low_s * hs)
        s_high, s_low = split(low_s * hc + low_c * hs)
        table_ref[:, part * 128 : (part + 1) * 128] = jnp.concatenate(
            [c_high, s_high, c_low, s_low], axis=0
        )
    total = jnp.zeros((4 * orders, rows), jnp.float32)
    for piece, copy in enumerate(large):
        copy.wait()
        at = slice(piece * width, (piece + 1) * width)
        total += lax.dot_general(
            table_ref[:, at],
            patch_ref[:, :, at].reshape(rows, width),
            NT,
            preferred_element_type=jnp.float32,
        )
    total = total[: 2 * orders] + total[2 * orders :]
    cosine, sine = total[:orders], total[orders:]
    real, imag = turn_c * cosine - turn_s * sine, -(turn_s * cosine + turn_c * sine)
    r_high, r_low = split(real)
    i_high, i_low = split(imag)
    stacked = jnp.concatenate([r_high, i_high, r_low, i_low], axis=0)
    summed = lax.dot_general(stacked, chosen, NT, preferred_element_type=jnp.float32)
    summed = summed[: 2 * orders] + summed[2 * orders :]
    real, imag = summed[:orders], summed[orders:]
    pieces = []
    for slot in range(m_dev):
        at = slice(slot * n_sim, (slot + 1) * n_sim)
        pieces += [real[at], imag[at]]
    value = jnp.concatenate(pieces, axis=1)
    for column in range(lax.axis_size("lens")):
        out_ref[:, column] = value


def fourier_terms(patches, patch_cycle, patch_block, m_values, shell_weight, scale):
    number, shells, bpx = patches.shape
    orders = m_values.shape[0]
    n_sim, n_lens = lax.axis_size("sim"), lax.axis_size("lens")
    small = [
        m_values.reshape(1, -1),
        patch_cycle.reshape(1, -1),
        patch_block.reshape(1, -1),
        shell_weight.reshape(1, -1),
    ]
    width = orders // n_sim * 2 * n_sim
    return pl.pallas_call(
        lambda *refs: terms_kernel(scale, *refs),
        out_shape=jax.ShapeDtypeStruct((n_sim, n_lens, width), jnp.float32),
        in_specs=[pl.BlockSpec(memory_space=pltpu.HBM)] * 5,
        out_specs=pl.BlockSpec(memory_space=pltpu.VMEM),
        scratch_shapes=[pltpu.VMEM(x.shape, x.dtype) for x in small]
        + [
            pltpu.VMEM(patches.shape, patches.dtype),
            pltpu.VMEM((4 * orders, bpx), jnp.bfloat16),
            pltpu.SemaphoreType.DMA((4,)),
            pltpu.SemaphoreType.DMA((PIECES,)),
        ],
        compiler_params=pltpu.CompilerParams(vmem_limit_bytes=48 << 20),
        name="fourier_terms",
    )(*[pltpu.with_memory_space_constraint(x, pltpu.HBM) for x in small + [patches]])


def finish_kernel(terms_ref, own_ref, spin_ref, *refs):
    other_refs, (kappa_ref, shear_ref) = refs[:-2], refs[-2:]
    m_dev, rows, lmax = own_ref.shape
    n_lens = lax.axis_size("lens")
    rank = lax.axis_index("lens")
    ell = iota((8, lmax), 1).astype(jnp.float32)
    factor = jnp.where(
        ell >= 2.0, jnp.sqrt((ell + 2.0) * (ell - 1.0) / jnp.maximum(ell * (ell + 1.0), 1.0)), 0.0
    )[0:1]
    steps = range(n_lens)
    modes = [jnp.sum(terms_ref[:, rank ^ step], axis=0, keepdims=True) for step in steps]
    same = iota((rows, rows), 0) == iota((rows, rows), 1)
    for slot in range(m_dev):
        columns = []
        for part in range(2):
            at = (slot * 2 + part) * rows
            columns.append(
                jnp.concatenate(
                    [
                        jnp.sum(jnp.where(same, m[:, at : at + rows], 0.0), axis=1, keepdims=True)
                        for m in modes
                    ],
                    axis=0,
                )
            )
        shear = (spin_ref[slot].astype(jnp.float32) * factor).astype(jnp.bfloat16)
        left = jnp.concatenate([own_ref[slot], shear], axis=0)
        right = jnp.concatenate([own_ref[slot]] + [r[slot] for r in other_refs], axis=0)
        gram = lax.dot_general(right, left, NT, preferred_element_type=jnp.float32)
        for part in range(2):
            both = jnp.sum(gram * columns[part], axis=0, keepdims=True)
            kappa_ref[slot, part : part + 1] = both[:, :rows]
            shear_ref[slot, part : part + 1] = both[:, rows:]


def finish(terms, own, spin, others):
    m_dev, rows, lmax = own.shape
    shape = jax.ShapeDtypeStruct((m_dev, 2, rows), jnp.float32)
    cycles = rows * (1 + len(others))
    return pl.pallas_call(
        finish_kernel,
        out_shape=(shape, shape),
        compiler_params=pltpu.CompilerParams(vmem_limit_bytes=48 << 20),
        cost_estimate=pl.CostEstimate(
            flops=4 * m_dev * rows * cycles * lmax,
            bytes_accessed=2 * own.size * (2 + len(others)),
            transcendentals=0,
        ),
        name="finish",
    )(terms, own, spin, *others)


def on_device(
    patches, patch_cycle, patch_block, m_values, shell_weight, legendre_panel, spin2_panel
):
    n_sim = lax.axis_size("sim")
    n_lens = lax.axis_size("lens")
    m_dev, rows, lmax = legendre_panel.shape
    axes = ("sim", "lens")

    def swap(x, mask):
        return lax.ppermute(x, axes, [(i, i ^ mask) for i in range(n_sim * n_lens)])

    others = [swap(legendre_panel, step) for step in range(1, n_lens)]
    scale = 1.0 / math.sqrt(NPIX * n_sim * n_lens * lmax)
    terms = fourier_terms(patches, patch_cycle, patch_block, m_values, shell_weight, scale)
    terms = terms.reshape(n_sim * n_lens, 1, -1)
    terms = lax.all_to_all(terms, axes, 0, 0, tiled=True)
    return finish(terms.reshape(n_sim, n_lens, -1), legendre_panel, spin2_panel, others)


def solution(mesh):
    placed = (
        P(("sim", "lens"), None, None),
        P(("sim", "lens"), None),
        P(("sim", "lens")),
        P(),
        P(),
        P("sim", "lens", None),
        P("sim", "lens", None),
    )
    return jax.shard_map(
        on_device,
        mesh=mesh,
        in_specs=placed,
        out_specs=(P("sim", None, "lens"), P("sim", None, "lens")),
        check_vma=False,
    )
```

```python
import math

import jax
import jax.numpy as jnp
from jax import lax
from jax.experimental import pallas as pl
from jax.experimental.pallas import tpu as pltpu
from jax.sharding import PartitionSpec as P

NPIX = 16384
NT = (((1,), (1,)), ((), ()))
PIECES = 1
GROUP = 8


def cos_sin(index, turn):
    quarter = turn // 4
    quadrant = (index + quarter // 2) // quarter
    r = (index - quadrant * quarter).astype(jnp.float32) * (2.0 * math.pi / turn)
    q = r * r
    sine = r + r * q * (-1.0 / 6 + q * (1.0 / 120 + q * (-1.0 / 5040 + q * (1.0 / 362880))))
    cosine = 1.0 + q * (-0.5 + q * (1.0 / 24 + q * (-1.0 / 720 + q * (1.0 / 40320))))
    odd = (quadrant & 1) == 1
    c = jnp.where(odd, sine, cosine)
    s = jnp.where(odd, cosine, sine)
    c = jnp.where(((quadrant + 1) & 2) == 2, -c, c)
    s = jnp.where((quadrant & 2) == 2, -s, s)
    return c, s


def split(x):
    high = x.astype(jnp.bfloat16)
    return high, (x - high.astype(jnp.float32)).astype(jnp.bfloat16)


def iota(shape, dim):
    return lax.broadcasted_iota(jnp.int32, shape, dim)


def terms_kernel(
    scale, m_hbm, cycle_hbm, block_hbm, weight_hbm, patch_hbm, out_ref,
    m_ref, cycle_ref, block_ref, weight_ref, patch_ref, small_sem, patch_sem
):
    number, shells, bpx = patch_ref.shape
    orders = m_ref.shape[1]
    n_sim = lax.axis_size("sim")
    m_dev = orders // n_sim
    small = [
        pltpu.make_async_copy(source, target, small_sem.at[i])
        for i, (source, target) in enumerate(
            ((m_hbm, m_ref), (cycle_hbm, cycle_ref), (block_hbm, block_ref), (weight_hbm, weight_ref))
        )
    ]
    width = bpx // PIECES
    large = [
        pltpu.make_async_copy(
            patch_hbm.at[:, :, pl.ds(i * width, width)],
            patch_ref.at[:, :, pl.ds(i * width, width)],
            patch_sem.at[i],
        )
        for i in range(PIECES)
    ]
    for copy in small + large:
        copy.start()
    square = (orders, orders)
    row = iota(square, 0)
    slot = (row % n_sim) * m_dev + row // n_sim
    for copy in small:
        copy.wait()
    m_row = m_ref[...].astype(jnp.float32)
    m_col = jnp.sum(jnp.where(slot == iota(square, 1), m_row, 0.0), axis=1, keepdims=True)
    m_col = m_col.astype(jnp.int32)
    low_c, low_s = cos_sin((m_col * iota((orders, 128), 1)) & (NPIX - 1), NPIX)
    parts = bpx // 128
    high_c, high_s = cos_sin((m_col * (128 * iota((orders, 128), 1))) & (NPIX - 1), NPIX)
    rows = number * shells
    where = jnp.where(iota((8, number), 0) == 0, block_ref[...], cycle_ref[...])
    spread = (iota((number, rows), 1) // shells == iota((number, rows), 0)).astype(jnp.bfloat16)
    where = jnp.dot(
        where.astype(jnp.float32).astype(jnp.bfloat16), spread, preferred_element_type=jnp.float32
    ).astype(jnp.int32)
    block, cycle = where[0:1], where[1:2]
    parity = (cycle + lax.axis_index("lens") * n_sim) & 1
    phase = 2 * bpx * block + parity
    turn_c, turn_s = cos_sin((m_col * phase) & (2 * NPIX - 1), 2 * NPIX)
    lane = iota((1, rows), 1) % shells
    weight = jnp.zeros((1, rows), jnp.float32)
    for shell in range(shells):
        weight = jnp.where(lane == shell, weight_ref[0:1, shell : shell + 1] * scale, weight)
    turn_c, turn_s = turn_c * weight, turn_s * weight
    chosen = (iota((n_sim, rows), 0) == cycle).astype(jnp.bfloat16)
    large[0].wait()
    total = jnp.zeros((4 * orders, rows), jnp.float32)
    for first in range(0, parts, GROUP):
        tables = []
        for part in range(first, first + GROUP):
            hc = high_c[:, part : part + 1]
            hs = high_s[:, part : part + 1]
            c_high, c_low = split(low_c * hc - low_s * hs)
            s_high, s_low = split(low_s * hc + low_c * hs)
            tables.append(jnp.concatenate([c_high, s_high, c_low, s_low], axis=0))
        chunk = patch_ref[:, :, first * 128 : (first + GROUP) * 128].reshape(rows, GROUP * 128)
        total += lax.dot_general(
            jnp.concatenate(tables, axis=1), chunk, NT, preferred_element_type=jnp.float32
        )
    total = total[: 2 * orders] + total[2 * orders :]
    cosine, sine = total[:orders], total[orders:]
    real, imag = turn_c * cosine - turn_s * sine, -(turn_s * cosine + turn_c * sine)
    r_high, r_low = split(real)
    i_high, i_low = split(imag)
    stacked = jnp.concatenate([r_high, i_high, r_low, i_low], axis=0)
    summed = lax.dot_general(stacked, chosen, NT, preferred_element_type=jnp.float32)
    summed = summed[: 2 * orders] + summed[2 * orders :]
    real, imag = summed[:orders], summed[orders:]
    pieces = []
    for slot in range(m_dev):
        at = slice(slot * n_sim, (slot + 1) * n_sim)
        pieces += [real[at], imag[at]]
    value = jnp.concatenate(pieces, axis=1)
    for column in range(lax.axis_size("lens")):
        out_ref[:, column] = value


def fourier_terms(patches, patch_cycle, patch_block, m_values, shell_weight, scale):
    number, shells, bpx = patches.shape
    orders = m_values.shape[0]
    n_sim, n_lens = lax.axis_size("sim"), lax.axis_size("lens")
    small = [
        m_values.reshape(1, -1),
        patch_cycle.reshape(1, -1),
        patch_block.reshape(1, -1),
        shell_weight.reshape(1, -1),
    ]
    width = orders // n_sim * 2 * n_sim
    return pl.pallas_call(
        lambda *refs: terms_kernel(scale, *refs),
        out_shape=jax.ShapeDtypeStruct((n_sim, n_lens, width), jnp.float32),
        in_specs=[pl.BlockSpec(memory_space=pltpu.HBM)] * 5,
        out_specs=pl.BlockSpec(memory_space=pltpu.VMEM),
        scratch_shapes=[pltpu.VMEM(x.shape, x.dtype) for x in small]
        + [
            pltpu.VMEM(patches.shape, patches.dtype),
            pltpu.SemaphoreType.DMA((4,)),
            pltpu.SemaphoreType.DMA((PIECES,)),
        ],
        compiler_params=pltpu.CompilerParams(vmem_limit_bytes=48 << 20),
        name="fourier_terms",
    )(*[pltpu.with_memory_space_constraint(x, pltpu.HBM) for x in small + [patches]])


def finish_kernel(terms_ref, own_ref, spin_ref, *refs):
    other_refs, (kappa_ref, shear_ref) = refs[:-2], refs[-2:]
    m_dev, rows, lmax = own_ref.shape
    n_lens = lax.axis_size("lens")
    rank = lax.axis_index("lens")
    ell = iota((8, lmax), 1).astype(jnp.float32)
    factor = jnp.where(
        ell >= 2.0, jnp.sqrt(1.0 - 2.0 / jnp.maximum(ell * (ell + 1.0), 2.0)), 0.0
    )[0:1]
    steps = range(n_lens)
    modes = [jnp.sum(terms_ref[:, rank ^ step], axis=0, keepdims=True) for step in steps]
    same = iota((rows, rows), 0) == iota((rows, rows), 1)
    for slot in range(m_dev):
        columns = []
        for part in range(2):
            at = (slot * 2 + part) * rows
            columns.append(
                jnp.concatenate(
                    [
                        jnp.sum(jnp.where(same, m[:, at : at + rows], 0.0), axis=1, keepdims=True)
                        for m in modes
                    ],
                    axis=0,
                )
            )
        shear = (spin_ref[slot].astype(jnp.float32) * factor).astype(jnp.bfloat16)
        left = jnp.concatenate([own_ref[slot], shear], axis=0)
        right = jnp.concatenate([own_ref[slot]] + [r[slot] for r in other_refs], axis=0)
        gram = lax.dot_general(right, left, NT, preferred_element_type=jnp.float32)
        for part in range(2):
            both = jnp.sum(gram * columns[part], axis=0, keepdims=True)
            kappa_ref[slot, part : part + 1] = both[:, :rows]
            shear_ref[slot, part : part + 1] = both[:, rows:]


def finish(terms, own, spin, others):
    m_dev, rows, lmax = own.shape
    shape = jax.ShapeDtypeStruct((m_dev, 2, rows), jnp.float32)
    cycles = rows * (1 + len(others))
    return pl.pallas_call(
        finish_kernel,
        out_shape=(shape, shape),
        compiler_params=pltpu.CompilerParams(vmem_limit_bytes=48 << 20),
        cost_estimate=pl.CostEstimate(
            flops=4 * m_dev * rows * cycles * lmax,
            bytes_accessed=2 * own.size * (2 + len(others)),
            transcendentals=0,
        ),
        name="finish",
    )(terms, own, spin, *others)


def on_device(
    patches, patch_cycle, patch_block, m_values, shell_weight, legendre_panel, spin2_panel
):
    n_sim = lax.axis_size("sim")
    n_lens = lax.axis_size("lens")
    m_dev, rows, lmax = legendre_panel.shape
    axes = ("sim", "lens")

    def swap(x, mask):
        return lax.ppermute(x, axes, [(i, i ^ mask) for i in range(n_sim * n_lens)])

    others = [swap(legendre_panel, step) for step in range(1, n_lens)]
    scale = 1.0 / math.sqrt(NPIX * n_sim * n_lens * lmax)
    terms = fourier_terms(patches, patch_cycle, patch_block, m_values, shell_weight, scale)
    terms = terms.reshape(n_sim * n_lens, 1, -1)
    terms = lax.all_to_all(terms, axes, 0, 0, tiled=True)
    return finish(terms.reshape(n_sim, n_lens, -1), legendre_panel, spin2_panel, others)


def solution(mesh):
    placed = (
        P(("sim", "lens"), None, None),
        P(("sim", "lens"), None),
        P(("sim", "lens")),
        P(),
        P(),
        P("sim", "lens", None),
        P("sim", "lens", None),
    )
    return jax.shard_map(
        on_device,
        mesh=mesh,
        in_specs=placed,
        out_specs=(P("sim", None, "lens"), P("sim", None, "lens")),
        check_vma=False,
    )
```

```python
import math

import jax
import jax.numpy as jnp
from jax import lax
from jax.experimental import pallas as pl
from jax.experimental.pallas import tpu as pltpu
from jax.sharding import PartitionSpec as P

NPIX = 16384
NT = (((1,), (1,)), ((), ()))
PIECES = 1
GROUP = 8


def cos_sin(index, turn):
    quarter = turn // 4
    quadrant = (index + quarter // 2) // quarter
    r = (index - quadrant * quarter).astype(jnp.float32) * (2.0 * math.pi / turn)
    q = r * r
    sine = r + r * q * (-1.0 / 6 + q * (1.0 / 120 + q * (-1.0 / 5040 + q * (1.0 / 362880))))
    cosine = 1.0 + q * (-0.5 + q * (1.0 / 24 + q * (-1.0 / 720 + q * (1.0 / 40320))))
    odd = (quadrant & 1) == 1
    c = jnp.where(odd, sine, cosine)
    s = jnp.where(odd, cosine, sine)
    c = jnp.where(((quadrant + 1) & 2) == 2, -c, c)
    s = jnp.where((quadrant & 2) == 2, -s, s)
    return c, s


def split(x):
    high = x.astype(jnp.bfloat16)
    return high, (x - high.astype(jnp.float32)).astype(jnp.bfloat16)


def iota(shape, dim):
    return lax.broadcasted_iota(jnp.int32, shape, dim)


def terms_kernel(
    scale, m_hbm, cycle_hbm, block_hbm, weight_hbm, patch_hbm, own_hbm, spin_hbm,
    out_ref, own_ref, spin_ref, m_ref, cycle_ref, block_ref, weight_ref, patch_ref, small_sem, patch_sem, panel_sem
):
    number, shells, bpx = patch_ref.shape
    orders = m_ref.shape[1]
    n_sim = lax.axis_size("sim")
    m_dev = orders // n_sim
    small = [
        pltpu.make_async_copy(source, target, small_sem.at[i])
        for i, (source, target) in enumerate(
            ((m_hbm, m_ref), (cycle_hbm, cycle_ref), (block_hbm, block_ref), (weight_hbm, weight_ref))
        )
    ]
    width = bpx // PIECES
    large = [
        pltpu.make_async_copy(
            patch_hbm.at[:, :, pl.ds(i * width, width)],
            patch_ref.at[:, :, pl.ds(i * width, width)],
            patch_sem.at[i],
        )
        for i in range(PIECES)
    ]
    for copy in small + large:
        copy.start()
    square = (orders, orders)
    row = iota(square, 0)
    slot = (row % n_sim) * m_dev + row // n_sim
    for copy in small:
        copy.wait()
    panels = [
        pltpu.make_async_copy(source, target, panel_sem.at[i])
        for i, (source, target) in enumerate(((own_hbm, own_ref), (spin_hbm, spin_ref)))
    ]
    m_row = m_ref[...].astype(jnp.float32)
    m_col = jnp.sum(jnp.where(slot == iota(square, 1), m_row, 0.0), axis=1, keepdims=True)
    m_col = m_col.astype(jnp.int32)
    low_c, low_s = cos_sin((m_col * iota((orders, 128), 1)) & (NPIX - 1), NPIX)
    parts = bpx // 128
    high_c, high_s = cos_sin((m_col * (128 * iota((orders, 128), 1))) & (NPIX - 1), NPIX)
    rows = number * shells
    where = jnp.where(iota((8, number), 0) == 0, block_ref[...], cycle_ref[...])
    spread = (iota((number, rows), 1) // shells == iota((number, rows), 0)).astype(jnp.bfloat16)
    where = jnp.dot(
        where.astype(jnp.float32).astype(jnp.bfloat16), spread, preferred_element_type=jnp.float32
    ).astype(jnp.int32)
    block, cycle = where[0:1], where[1:2]
    parity = (cycle + lax.axis_index("lens") * n_sim) & 1
    phase = 2 * bpx * block + parity
    turn_c, turn_s = cos_sin((m_col * phase) & (2 * NPIX - 1), 2 * NPIX)
    lane = iota((1, rows), 1) % shells
    weight = jnp.zeros((1, rows), jnp.float32)
    for shell in range(shells):
        weight = jnp.where(lane == shell, weight_ref[0:1, shell : shell + 1] * scale, weight)
    turn_c, turn_s = turn_c * weight, turn_s * weight
    chosen = (iota((n_sim, rows), 0) == cycle).astype(jnp.bfloat16)
    for copy in panels:
        copy.start()
    large[0].wait()
    total = jnp.zeros((4 * orders, rows), jnp.float32)
    for first in range(0, parts, GROUP):
        tables = []
        for part in range(first, first + GROUP):
            hc = high_c[:, part : part + 1]
            hs = high_s[:, part : part + 1]
            c_high, c_low = split(low_c * hc - low_s * hs)
            s_high, s_low = split(low_s * hc + low_c * hs)
            tables.append(jnp.concatenate([c_high, s_high, c_low, s_low], axis=0))
        chunk = patch_ref[:, :, first * 128 : (first + GROUP) * 128].reshape(rows, GROUP * 128)
        total += lax.dot_general(
            jnp.concatenate(tables, axis=1), chunk, NT, preferred_element_type=jnp.float32
        )
    total = total[: 2 * orders] + total[2 * orders :]
    cosine, sine = total[:orders], total[orders:]
    real, imag = turn_c * cosine - turn_s * sine, -(turn_s * cosine + turn_c * sine)
    r_high, r_low = split(real)
    i_high, i_low = split(imag)
    stacked = jnp.concatenate([r_high, i_high, r_low, i_low], axis=0)
    summed = lax.dot_general(stacked, chosen, NT, preferred_element_type=jnp.float32)
    summed = summed[: 2 * orders] + summed[2 * orders :]
    real, imag = summed[:orders], summed[orders:]
    pieces = []
    for slot in range(m_dev):
        at = slice(slot * n_sim, (slot + 1) * n_sim)
        pieces += [real[at], imag[at]]
    value = jnp.concatenate(pieces, axis=1)
    for column in range(lax.axis_size("lens")):
        out_ref[:, column] = value
    for copy in panels:
        copy.wait()


def fourier_terms(
    patches, patch_cycle, patch_block, m_values, shell_weight, own, spin, scale
):
    number, shells, bpx = patches.shape
    orders = m_values.shape[0]
    n_sim, n_lens = lax.axis_size("sim"), lax.axis_size("lens")
    small = [
        m_values.reshape(1, -1),
        patch_cycle.reshape(1, -1),
        patch_block.reshape(1, -1),
        shell_weight.reshape(1, -1),
    ]
    width = orders // n_sim * 2 * n_sim
    return pl.pallas_call(
        lambda *refs: terms_kernel(scale, *refs),
        out_shape=(
            jax.ShapeDtypeStruct((n_sim, n_lens, width), jnp.float32),
            jax.ShapeDtypeStruct(own.shape, own.dtype),
            jax.ShapeDtypeStruct(spin.shape, spin.dtype),
        ),
        in_specs=[pl.BlockSpec(memory_space=pltpu.HBM)] * 7,
        out_specs=[pl.BlockSpec(memory_space=pltpu.VMEM)] * 3,
        scratch_shapes=[pltpu.VMEM(x.shape, x.dtype) for x in small]
        + [
            pltpu.VMEM(patches.shape, patches.dtype),
            pltpu.SemaphoreType.DMA((4,)),
            pltpu.SemaphoreType.DMA((PIECES,)),
            pltpu.SemaphoreType.DMA((2,)),
        ],
        compiler_params=pltpu.CompilerParams(vmem_limit_bytes=48 << 20),
        name="fourier_terms",
    )(*[pltpu.with_memory_space_constraint(x, pltpu.HBM) for x in small + [patches, own, spin]])


def finish_kernel(terms_ref, own_ref, spin_ref, *refs):
    other_refs, (kappa_ref, shear_ref) = refs[:-2], refs[-2:]
    m_dev, rows, lmax = own_ref.shape
    n_lens = lax.axis_size("lens")
    rank = lax.axis_index("lens")
    ell = iota((8, lmax), 1).astype(jnp.float32)
    factor = jnp.where(
        ell >= 2.0, jnp.sqrt(1.0 - 2.0 / jnp.maximum(ell * (ell + 1.0), 2.0)), 0.0
    )[0:1]
    steps = range(n_lens)
    modes = [jnp.sum(terms_ref[:, rank ^ step], axis=0, keepdims=True) for step in steps]
    same = iota((rows, rows), 0) == iota((rows, rows), 1)
    for slot in range(m_dev):
        columns = []
        for part in range(2):
            at = (slot * 2 + part) * rows
            columns.append(
                jnp.concatenate(
                    [
                        jnp.sum(jnp.where(same, m[:, at : at + rows], 0.0), axis=1, keepdims=True)
                        for m in modes
                    ],
                    axis=0,
                )
            )
        shear = (spin_ref[slot].astype(jnp.float32) * factor).astype(jnp.bfloat16)
        left = jnp.concatenate([own_ref[slot], shear], axis=0)
        right = jnp.concatenate([own_ref[slot]] + [r[slot] for r in other_refs], axis=0)
        gram = lax.dot_general(right, left, NT, preferred_element_type=jnp.float32)
        for part in range(2):
            both = jnp.sum(gram * columns[part], axis=0, keepdims=True)
            kappa_ref[slot, part : part + 1] = both[:, :rows]
            shear_ref[slot, part : part + 1] = both[:, rows:]


def finish(terms, own, spin, others):
    m_dev, rows, lmax = own.shape
    shape = jax.ShapeDtypeStruct((m_dev, 2, rows), jnp.float32)
    cycles = rows * (1 + len(others))
    return pl.pallas_call(
        finish_kernel,
        out_shape=(shape, shape),
        compiler_params=pltpu.CompilerParams(vmem_limit_bytes=48 << 20),
        cost_estimate=pl.CostEstimate(
            flops=4 * m_dev * rows * cycles * lmax,
            bytes_accessed=2 * own.size * (2 + len(others)),
            transcendentals=0,
        ),
        name="finish",
    )(terms, own, spin, *others)


def on_device(
    patches, patch_cycle, patch_block, m_values, shell_weight, legendre_panel, spin2_panel
):
    n_sim = lax.axis_size("sim")
    n_lens = lax.axis_size("lens")
    m_dev, rows, lmax = legendre_panel.shape
    axes = ("sim", "lens")

    def swap(x, mask):
        return lax.ppermute(x, axes, [(i, i ^ mask) for i in range(n_sim * n_lens)])

    others = [swap(legendre_panel, step) for step in range(1, n_lens)]
    scale = 1.0 / math.sqrt(NPIX * n_sim * n_lens * lmax)
    terms, own, spin = fourier_terms(
        patches,
        patch_cycle,
        patch_block,
        m_values,
        shell_weight,
        legendre_panel,
        spin2_panel,
        scale,
    )
    terms = terms.reshape(n_sim * n_lens, 1, -1)
    terms = lax.all_to_all(terms, axes, 0, 0, tiled=True)
    return finish(terms.reshape(n_sim, n_lens, -1), own, spin, others)


def solution(mesh):
    placed = (
        P(("sim", "lens"), None, None),
        P(("sim", "lens"), None),
        P(("sim", "lens")),
        P(),
        P(),
        P("sim", "lens", None),
        P("sim", "lens", None),
    )
    return jax.shard_map(
        on_device,
        mesh=mesh,
        in_specs=placed,
        out_specs=(P("sim", None, "lens"), P("sim", None, "lens")),
        check_vma=False,
    )
```

```python
import math

import jax
import jax.numpy as jnp
from jax import lax
from jax.experimental import pallas as pl
from jax.experimental.pallas import tpu as pltpu
from jax.sharding import PartitionSpec as P

NPIX = 16384
NT = (((1,), (1,)), ((), ()))
PIECES = 1
GROUP = 8


def cos_sin(index, turn):
    quarter = turn // 4
    quadrant = (index + quarter // 2) // quarter
    r = (index - quadrant * quarter).astype(jnp.float32) * (2.0 * math.pi / turn)
    q = r * r
    sine = r + r * q * (-1.0 / 6 + q * (1.0 / 120 + q * (-1.0 / 5040 + q * (1.0 / 362880))))
    cosine = 1.0 + q * (-0.5 + q * (1.0 / 24 + q * (-1.0 / 720 + q * (1.0 / 40320))))
    odd = (quadrant & 1) == 1
    c = jnp.where(odd, sine, cosine)
    s = jnp.where(odd, cosine, sine)
    c = jnp.where(((quadrant + 1) & 2) == 2, -c, c)
    s = jnp.where((quadrant & 2) == 2, -s, s)
    return c, s


def split(x):
    high = x.astype(jnp.bfloat16)
    return high, (x - high.astype(jnp.float32)).astype(jnp.bfloat16)


def iota(shape, dim):
    return lax.broadcasted_iota(jnp.int32, shape, dim)


def terms_kernel(
    scale, m_hbm, cycle_hbm, block_hbm, weight_hbm, patch_hbm, own_hbm, spin_hbm,
    out_ref, own_ref, spin_ref, factor_ref, m_ref, cycle_ref, block_ref, weight_ref, patch_ref, small_sem, patch_sem, panel_sem
):
    number, shells, bpx = patch_ref.shape
    orders = m_ref.shape[1]
    n_sim = lax.axis_size("sim")
    m_dev = orders // n_sim
    small = [
        pltpu.make_async_copy(source, target, small_sem.at[i])
        for i, (source, target) in enumerate(
            ((m_hbm, m_ref), (cycle_hbm, cycle_ref), (block_hbm, block_ref), (weight_hbm, weight_ref))
        )
    ]
    width = bpx // PIECES
    large = [
        pltpu.make_async_copy(
            patch_hbm.at[:, :, pl.ds(i * width, width)],
            patch_ref.at[:, :, pl.ds(i * width, width)],
            patch_sem.at[i],
        )
        for i in range(PIECES)
    ]
    for copy in small + large:
        copy.start()
    ell = iota(factor_ref.shape, 1).astype(jnp.float32)
    below = jnp.sqrt(1.0 - 2.0 / jnp.maximum(ell * (ell + 1.0), 2.0))
    factor_ref[...] = jnp.where(ell >= 2.0, below, 0.0)
    square = (orders, orders)
    row = iota(square, 0)
    slot = (row % n_sim) * m_dev + row // n_sim
    for copy in small:
        copy.wait()
    panels = [
        pltpu.make_async_copy(source, target, panel_sem.at[i])
        for i, (source, target) in enumerate(((own_hbm, own_ref), (spin_hbm, spin_ref)))
    ]
    m_row = m_ref[...].astype(jnp.float32)
    m_col = jnp.sum(jnp.where(slot == iota(square, 1), m_row, 0.0), axis=1, keepdims=True)
    m_col = m_col.astype(jnp.int32)
    low_c, low_s = cos_sin((m_col * iota((orders, 128), 1)) & (NPIX - 1), NPIX)
    parts = bpx // 128
    high_c, high_s = cos_sin((m_col * (128 * iota((orders, 128), 1))) & (NPIX - 1), NPIX)
    rows = number * shells
    where = jnp.where(iota((8, number), 0) == 0, block_ref[...], cycle_ref[...])
    spread = (iota((number, rows), 1) // shells == iota((number, rows), 0)).astype(jnp.bfloat16)
    where = jnp.dot(
        where.astype(jnp.float32).astype(jnp.bfloat16), spread, preferred_element_type=jnp.float32
    ).astype(jnp.int32)
    block, cycle = where[0:1], where[1:2]
    parity = (cycle + lax.axis_index("lens") * n_sim) & 1
    phase = 2 * bpx * block + parity
    turn_c, turn_s = cos_sin((m_col * phase) & (2 * NPIX - 1), 2 * NPIX)
    lane = iota((1, rows), 1) % shells
    weight = jnp.zeros((1, rows), jnp.float32)
    for shell in range(shells):
        weight = jnp.where(lane == shell, weight_ref[0:1, shell : shell + 1] * scale, weight)
    turn_c, turn_s = turn_c * weight, turn_s * weight
    chosen = (iota((n_sim, rows), 0) == cycle).astype(jnp.bfloat16)
    for copy in panels:
        copy.start()
    large[0].wait()
    total = jnp.zeros((4 * orders, rows), jnp.float32)
    for first in range(0, parts, GROUP):
        tables = []
        for part in range(first, first + GROUP):
            hc = high_c[:, part : part + 1]
            hs = high_s[:, part : part + 1]
            c_high, c_low = split(low_c * hc - low_s * hs)
            s_high, s_low = split(low_s * hc + low_c * hs)
            tables.append(jnp.concatenate([c_high, s_high, c_low, s_low], axis=0))
        chunk = patch_ref[:, :, first * 128 : (first + GROUP) * 128].reshape(rows, GROUP * 128)
        total += lax.dot_general(
            jnp.concatenate(tables, axis=1), chunk, NT, preferred_element_type=jnp.float32
        )
    total = total[: 2 * orders] + total[2 * orders :]
    cosine, sine = total[:orders], total[orders:]
    real, imag = turn_c * cosine - turn_s * sine, -(turn_s * cosine + turn_c * sine)
    r_high, r_low = split(real)
    i_high, i_low = split(imag)
    stacked = jnp.concatenate([r_high, i_high, r_low, i_low], axis=0)
    summed = lax.dot_general(stacked, chosen, NT, preferred_element_type=jnp.float32)
    summed = summed[: 2 * orders] + summed[2 * orders :]
    real, imag = summed[:orders], summed[orders:]
    pieces = []
    for slot in range(m_dev):
        at = slice(slot * n_sim, (slot + 1) * n_sim)
        pieces += [real[at], imag[at]]
    value = jnp.concatenate(pieces, axis=1)
    for column in range(lax.axis_size("lens")):
        out_ref[:, column] = value
    for copy in panels:
        copy.wait()


def fourier_terms(
    patches, patch_cycle, patch_block, m_values, shell_weight, own, spin, scale
):
    number, shells, bpx = patches.shape
    orders = m_values.shape[0]
    n_sim, n_lens = lax.axis_size("sim"), lax.axis_size("lens")
    small = [
        m_values.reshape(1, -1),
        patch_cycle.reshape(1, -1),
        patch_block.reshape(1, -1),
        shell_weight.reshape(1, -1),
    ]
    width = orders // n_sim * 2 * n_sim
    return pl.pallas_call(
        lambda *refs: terms_kernel(scale, *refs),
        out_shape=(
            jax.ShapeDtypeStruct((n_sim, n_lens, width), jnp.float32),
            jax.ShapeDtypeStruct(own.shape, own.dtype),
            jax.ShapeDtypeStruct(spin.shape, spin.dtype),
            jax.ShapeDtypeStruct((8, own.shape[2]), jnp.float32),
        ),
        in_specs=[pl.BlockSpec(memory_space=pltpu.HBM)] * 7,
        out_specs=[pl.BlockSpec(memory_space=pltpu.VMEM)] * 4,
        scratch_shapes=[pltpu.VMEM(x.shape, x.dtype) for x in small]
        + [
            pltpu.VMEM(patches.shape, patches.dtype),
            pltpu.SemaphoreType.DMA((4,)),
            pltpu.SemaphoreType.DMA((PIECES,)),
            pltpu.SemaphoreType.DMA((2,)),
        ],
        compiler_params=pltpu.CompilerParams(vmem_limit_bytes=48 << 20),
        name="fourier_terms",
    )(*[pltpu.with_memory_space_constraint(x, pltpu.HBM) for x in small + [patches, own, spin]])


def make_grams(factor_ref, own_ref, spin_ref, other_refs, gram_ref):
    for slot in range(own_ref.shape[0]):
        shear = (spin_ref[slot].astype(jnp.float32) * factor_ref[0:1]).astype(jnp.bfloat16)
        left = jnp.concatenate([own_ref[slot], shear], axis=0)
        right = jnp.concatenate([own_ref[slot]] + [r[slot] for r in other_refs], axis=0)
        gram_ref[slot] = lax.dot_general(right, left, NT, preferred_element_type=jnp.float32)


def waits_longest():
    return lax.axis_index("sim") == 0


def gram_kernel(factor_ref, own_ref, spin_ref, *refs):
    @pl.when(waits_longest())
    def _():
        make_grams(factor_ref, own_ref, spin_ref, refs[:-1], refs[-1])


def finish_kernel(terms_ref, ahead_ref, factor_ref, own_ref, spin_ref, *refs):
    other_refs, (kappa_ref, shear_ref, gram_ref) = refs[:-3], refs[-3:]
    m_dev, rows, lmax = own_ref.shape
    n_lens = lax.axis_size("lens")
    rank = lax.axis_index("lens")
    steps = range(n_lens)

    @pl.when(waits_longest())
    def _():
        gram_ref[...] = ahead_ref[...]

    @pl.when(jnp.logical_not(waits_longest()))
    def _():
        make_grams(factor_ref, own_ref, spin_ref, other_refs, gram_ref)

    modes = [jnp.sum(terms_ref[:, rank ^ step], axis=0, keepdims=True) for step in steps]
    turned = [jnp.broadcast_to(m, (8, m.shape[1])).T for m in modes]
    for slot in range(m_dev):
        gram = gram_ref[slot]
        for part in range(2):
            at = (slot * 2 + part) * rows
            column = jnp.concatenate([t[at : at + rows, 0:1] for t in turned], axis=0)
            both = jnp.sum(gram * column, axis=0, keepdims=True)
            kappa_ref[slot, part : part + 1] = both[:, :rows]
            shear_ref[slot, part : part + 1] = both[:, rows:]


def gram_shape(own, others):
    m_dev, rows, _ = own.shape
    return m_dev, rows * (1 + len(others)), 2 * rows


def grams_ahead(factor, own, spin, others):
    return pl.pallas_call(
        gram_kernel,
        out_shape=jax.ShapeDtypeStruct(gram_shape(own, others), jnp.float32),
        compiler_params=pltpu.CompilerParams(vmem_limit_bytes=48 << 20),
        name="grams_ahead",
    )(factor, own, spin, *others)


def finish(terms, grams, factor, own, spin, others):
    m_dev, rows, lmax = own.shape
    shape = jax.ShapeDtypeStruct((m_dev, 2, rows), jnp.float32)
    return pl.pallas_call(
        finish_kernel,
        out_shape=(shape, shape),
        scratch_shapes=[pltpu.VMEM(gram_shape(own, others), jnp.float32)],
        compiler_params=pltpu.CompilerParams(vmem_limit_bytes=48 << 20),
        name="finish",
    )(terms, grams, factor, own, spin, *others)


def on_device(
    patches, patch_cycle, patch_block, m_values, shell_weight, legendre_panel, spin2_panel
):
    n_sim = lax.axis_size("sim")
    n_lens = lax.axis_size("lens")
    m_dev, rows, lmax = legendre_panel.shape
    axes = ("sim", "lens")

    def swap(x, mask):
        return lax.ppermute(x, axes, [(i, i ^ mask) for i in range(n_sim * n_lens)])

    others = [swap(legendre_panel, step) for step in range(1, n_lens)]
    scale = 1.0 / math.sqrt(NPIX * n_sim * n_lens * lmax)
    terms, own, spin, factor = fourier_terms(
        patches,
        patch_cycle,
        patch_block,
        m_values,
        shell_weight,
        legendre_panel,
        spin2_panel,
        scale,
    )
    grams = grams_ahead(factor, own, spin, others)
    terms, grams = lax.optimization_barrier((terms, grams))
    terms = terms.reshape(n_sim * n_lens, 1, -1)
    terms = lax.all_to_all(terms, axes, 0, 0, tiled=True)
    return finish(terms.reshape(n_sim, n_lens, -1), grams, factor, own, spin, others)


def solution(mesh):
    placed = (
        P(("sim", "lens"), None, None),
        P(("sim", "lens"), None),
        P(("sim", "lens")),
        P(),
        P(),
        P("sim", "lens", None),
        P("sim", "lens", None),
    )
    return jax.shard_map(
        on_device,
        mesh=mesh,
        in_specs=placed,
        out_specs=(P("sim", None, "lens"), P("sim", None, "lens")),
        check_vma=False,
    )
```
